256 devices in a mesh: frame: 8 (over y, core), row: 4 (over z_lo), col: 8 (over z_hi, x).
Axes of the slice: x: 4, y: 4, z: 8 (z_hi: 2, z_lo: 4; z = z_hi * 4 + z_lo), core: 2. Of those that a mesh axis runs over, the one named last changes fastest.
Arguments:
- queries: bfloat16 [8, 4, 8, 384, 256], P('frame', 'row', 'col'), may hold values from -8 to 8
- key_vectors: bfloat16 [8, 4, 8, 384, 256], P('frame', 'row', 'col'), may hold values from -8 to 8
- value_vectors: bfloat16 [8, 4, 8, 384, 256], P('frame', 'row', 'col'), may hold values from -6 to 6
- forward_out: bfloat16 [8, 4, 8, 384, 256], P('frame', 'row', 'col'), may hold values from -6 to 6
- cotangent: bfloat16 [8, 4, 8, 384, 256], P('frame', 'row', 'col'), may hold values from -48 to 48
- log_norm: float32 [8, 4, 8, 2, 384], P('frame', 'row', 'col'), may hold values from 5 to 14
Outputs:
- grad_queries: bfloat16 [8, 4, 8, 384, 256], P('frame', 'row', 'col')
- grad_keys: bfloat16 [8, 4, 8, 384, 256], P('frame', 'row', 'col')
- grad_values: bfloat16 [8, 4, 8, 384, 256], P('frame', 'row', 'col')
The draws below stay inside these ranges and needn't reach their ends.
All inputs are finite; a program needn't handle non-finite values.
Results may differ from the reference program's by a relative error of at most 0.006.
Values may be sent and summed in bfloat16 or wider, within the bound.
No kernel may reach another device: no remote copies, remote signals or barrier semaphores. Data moves between devices by JAX's collectives and lax.ppermute only.
A program may use at most 128 MiB of HBM per device.

```python
import jax
import jax.numpy as jnp
from jax import lax

HEADS = 2
TILE_F = 6
TILE_R = 8
TILE_C = 8
TILE_TOK = 384
WIDTH = 256
TILES_F = 8
TILES_R = 4
TILES_C = 8


def draw_log_norm(key, part):
    key = jax.random.fold_in(key, 11)
    tile_count = TILE_F * TILE_R * TILE_C
    centre = jnp.log(jnp.float32(27 * tile_count)) + 1.9
    shape = (TILES_F, TILES_R, TILES_C, HEADS, tile_count)
    return centre + jax.random.uniform(key, shape, jnp.float32, -1.0, 0.6)


def level_of(key, extent, cuts, smallest, high):
    level, own = 1.0, jax.random.fold_in(key, 6)
    for axis_at, shards_of in cuts:
        heights = jnp.exp(jax.random.uniform(jax.random.fold_in(own, axis_at), (shards_of,), jnp.float32, smallest / len(cuts), high / len(cuts)))
        level = level * jnp.repeat(heights, extent[axis_at] // shards_of).reshape([-1 if axis == axis_at else 1 for axis in range(len(extent))])
    return level


def noise(key, dims, scale, most, cuts=(), kind=jnp.bfloat16):
    result = jax.random.normal(key, dims, jnp.float32) * scale
    if len(cuts) > 0:
        result = level_of(key, dims, cuts, -0.22, 0.18) * result
    return jnp.clip(result, min=-most, max=most).astype(kind)


def setup_inputs(seed: int = 0) -> dict:
    seeds = jax.random.split(jax.random.key(seed), 7)
    return {
        "queries": noise(seeds[0], (TILES_F, TILES_R, TILES_C, TILE_TOK, WIDTH), 1.4, 8.0, ((0, 8), (1, 4), (2, 8))),
        "key_vectors": noise(seeds[1], (TILES_F, TILES_R, TILES_C, TILE_TOK, WIDTH), 1.4, 8.0, ((0, 8), (1, 4), (2, 8))),
        "value_vectors": noise(seeds[2], (TILES_F, TILES_R, TILES_C, TILE_TOK, WIDTH), 1.0, 6.0, ((0, 8), (1, 4), (2, 8))),
        "forward_out": noise(seeds[3], (TILES_F, TILES_R, TILES_C, TILE_TOK, WIDTH), 1.0, 6.0, ((0, 8), (1, 4), (2, 8))),
        "cotangent": noise(seeds[4], (TILES_F, TILES_R, TILES_C, TILE_TOK, WIDTH), 8.0, 48.0, ((0, 8), (1, 4), (2, 8))),
        "log_norm": draw_log_norm(jax.random.fold_in(seeds[6], 71), 0),
    }


def rounded(values_in):
    return lax.optimization_barrier(values_in.astype(jnp.bfloat16)).astype(jnp.float32)


def neighbours(padded, frame_at, row_at, col_at):
    starts = [frame_at, row_at, col_at] + [jnp.int32(0)] * (padded.ndim - 3)
    block = lax.dynamic_slice(padded, starts, (3, 3, 3) + padded.shape[3:])
    return block.reshape((27 * padded.shape[3],) + padded.shape[4:])


def window_valid(frame_at, row_at, col_at, tiles_f, tiles_r, tiles_c):
    offsets = jnp.arange(3, dtype=jnp.int32) - 1
    along_f = (frame_at + offsets >= 0) & (frame_at + offsets < tiles_f)
    along_r = (row_at + offsets >= 0) & (row_at + offsets < tiles_r)
    along_c = (col_at + offsets >= 0) & (col_at + offsets < tiles_c)
    joined = along_f[:, None, None] & along_r[None, :, None] & along_c[None, None, :]
    return joined.reshape(27)


def reference(queries, key_vectors, value_vectors, forward_out, cotangent, log_norm):
    tiles_f, tiles_r, tiles_c, tile_rows, width = queries.shape
    head_count = log_norm.shape[3]
    head_width = width // head_count
    score_scale = head_width ** -0.5
    flat_count = tiles_f * tiles_r * tiles_c

    def split_heads(array_in):
        return array_in.astype(jnp.float32).reshape(array_in.shape[:-1] + (head_count, head_width))

    row_delta = jnp.sum(split_heads(cotangent) * split_heads(forward_out), axis=-1)
    log_rows = jnp.transpose(log_norm, (0, 1, 2, 4, 3))

    def padded(array_in):
        return jnp.pad(array_in, ((1, 1), (1, 1), (1, 1)) + ((0, 0),) * (array_in.ndim - 3))

    pad_q, pad_k, pad_v, pad_do = padded(queries), padded(key_vectors), padded(value_vectors), padded(cotangent)
    pad_log, pad_delta = padded(log_rows), padded(row_delta)
    flat_q = queries.reshape(flat_count, tile_rows, width)
    flat_k = key_vectors.reshape(flat_count, tile_rows, width)
    flat_v = value_vectors.reshape(flat_count, tile_rows, width)
    flat_do = cotangent.reshape(flat_count, tile_rows, width)
    flat_log = log_rows.reshape(flat_count, tile_rows, head_count)
    flat_delta = row_delta.reshape(flat_count, tile_rows, head_count)

    def one_tile(index):
        frame_at = index // (tiles_r * tiles_c)
        row_at = (index // tiles_c) % tiles_r
        col_at = index % tiles_c
        valid = jnp.repeat(window_valid(frame_at, row_at, col_at, tiles_f, tiles_r, tiles_c), tile_rows)
        own_q = split_heads(flat_q[index])
        own_k = split_heads(flat_k[index])
        own_v = split_heads(flat_v[index])
        own_do = split_heads(flat_do[index])
        own_log = flat_log[index]
        own_delta = flat_delta[index]
        near_q = split_heads(neighbours(pad_q, frame_at, row_at, col_at))
        near_k = split_heads(neighbours(pad_k, frame_at, row_at, col_at))
        near_v = split_heads(neighbours(pad_v, frame_at, row_at, col_at))
        near_do = split_heads(neighbours(pad_do, frame_at, row_at, col_at))
        near_log = neighbours(pad_log, frame_at, row_at, col_at)
        near_delta = neighbours(pad_delta, frame_at, row_at, col_at)

        scores = jnp.einsum('qhd,khd->hqk', own_q, near_k) * score_scale
        probs = jnp.where(valid[None, None, :], jnp.exp(scores - own_log.T[:, :, None]), 0.0)
        dprobs = jnp.einsum('qhd,khd->hqk', own_do, near_v)
        dscores = probs * (dprobs - own_delta.T[:, :, None])
        grad_q = jnp.einsum('hqk,khd->qhd', rounded(dscores), near_k) * score_scale

        scores_k = jnp.einsum('qhd,khd->hqk', near_q, own_k) * score_scale
        probs_k = jnp.where(valid[None, :, None], jnp.exp(scores_k - near_log.T[:, :, None]), 0.0)
        dprobs_k = jnp.einsum('qhd,khd->hqk', near_do, own_v)
        dscores_k = probs_k * (dprobs_k - near_delta.T[:, :, None])
        grad_v = jnp.einsum('hqk,qhd->khd', rounded(probs_k), near_do)
        grad_k = jnp.einsum('hqk,qhd->khd', rounded(dscores_k), near_q) * score_scale
        return (grad_q.reshape(tile_rows, width).astype(jnp.bfloat16),
                grad_k.reshape(tile_rows, width).astype(jnp.bfloat16),
                grad_v.reshape(tile_rows, width).astype(jnp.bfloat16))

    grads_q, grads_k, grads_v = lax.map(one_tile, jnp.arange(flat_count, dtype=jnp.int32))
    full_shape = (tiles_f, tiles_r, tiles_c, tile_rows, width)
    return grads_q.reshape(full_shape), grads_k.reshape(full_shape), grads_v.reshape(full_shape)
```

```python
import functools

import jax
import jax.numpy as jnp
from jax import lax
from jax.experimental import pallas as pl
from jax.experimental.pallas import tpu as pltpu
from jax.sharding import PartitionSpec as P

F32 = jnp.float32
BF16 = jnp.bfloat16
NT = (((1,), (1,)), ((), ()))
NN = (((1,), (0,)), ((), ()))
LANES = 128
VMEM_BYTES = 48 * 2**20


def dot(a, b, dims=NN):
    return lax.dot_general(a, b, dims, preferred_element_type=F32)


def shift(x, axis, by):
    peers = lax.axis_size(axis)
    pairs = [(i, i + by) for i in range(peers) if 0 <= i + by < peers]
    return lax.ppermute(x, axis, pairs)


def payload_kernel(heads, q_ref, do_ref, o_ref, log_ref, pay_ref):
    rows = q_ref.shape[0]
    blocks = rows // LANES
    for h in range(heads):
        cols = slice(h * LANES, (h + 1) * LANES)
        pay_ref[h * rows:(h + 1) * rows, :] = q_ref[:, cols]
        pay_ref[(heads + h) * rows:(heads + h + 1) * rows, :] = do_ref[:, cols]
    products = do_ref[...].astype(F32) * o_ref[...].astype(F32)
    turned = products.T
    parts = []
    for h in range(heads):
        parts += [log_ref[h:h + 1, j * LANES:(j + 1) * LANES] for j in range(blocks)]
    for h in range(heads):
        delta = jnp.sum(turned[h * LANES:(h + 1) * LANES], axis=0, keepdims=True)
        parts += [delta[:, j * LANES:(j + 1) * LANES] for j in range(blocks)]
    parts.append(jnp.zeros((16 - len(parts), LANES), F32))
    rest = jnp.concatenate(parts, axis=0)
    at = 2 * heads * rows
    for piece in range(3):
        low = rest.astype(BF16)
        pay_ref[at + 16 * piece:at + 16 * (piece + 1), :] = low
        rest = rest - low.astype(F32)


def make_payload(q, do, o, log_norm):
    rows, width = q.shape
    heads = log_norm.shape[0]
    return pl.pallas_call(
        functools.partial(payload_kernel, heads),
        out_shape=jax.ShapeDtypeStruct((2 * heads * rows + 48, LANES), BF16),
        compiler_params=pltpu.CompilerParams(vmem_limit_bytes=VMEM_BYTES),
        name="payload",
    )(q, do, o, log_norm)


def tiles_kernel(count, heads, scale, *refs):
    pays = refs[:count]
    k_ref, v_ref, dk_in, dv_in = refs[count:count + 4]
    dqs = refs[count + 4:2 * count + 4]
    dk_ref, dv_ref, kt_ref = refs[2 * count + 4:]
    rows = k_ref.shape[0]
    blocks = rows // LANES

    @pl.when(pl.program_id(0) == 0)
    def _():
        dk_ref[...] = dk_in[...]
        dv_ref[...] = dv_in[...]
        kt_ref[...] = k_ref[...].astype(F32).T.astype(BF16)

    def row_of(aux, kind):
        return jnp.concatenate([aux[kind * blocks + j:kind * blocks + j + 1] for j in range(blocks)], axis=1)

    at = 2 * heads * rows
    auxes = []
    for pay in pays:
        aux = pay[0, at:, :].astype(F32)
        auxes.append(aux[0:16] + aux[16:32] + aux[32:48])
    for h in range(heads):
        cols = slice(h * LANES, (h + 1) * LANES)
        k = k_ref[:, cols]
        v = v_ref[:, cols]
        all_p, all_ds = [], []
        for pay, aux in zip(pays, auxes):
            q = pay[0, h * rows:(h + 1) * rows, :]
            do = pay[0, (heads + h) * rows:(heads + h + 1) * rows, :]
            p = jnp.exp(dot(k, q, NT) * scale - row_of(aux, h))
            ds = p * (dot(v, do, NT) - row_of(aux, heads + h))
            all_p.append(p.astype(BF16))
            all_ds.append(ds.astype(BF16))
        p = jnp.concatenate(all_p, axis=1)
        ds = jnp.concatenate(all_ds, axis=1)
        q = jnp.concatenate([pay[0, h * rows:(h + 1) * rows, :] for pay in pays], axis=0)
        do = jnp.concatenate([pay[0, (heads + h) * rows:(heads + h + 1) * rows, :] for pay in pays], axis=0)
        dv_ref[:, cols] += dot(p, do)
        dk_ref[:, cols] += dot(ds, q)
        dq = dot(kt_ref[cols, :], ds)
        for i, dq_ref in enumerate(dqs):
            dq_ref[0, cols, :] = dq[:, i * rows:(i + 1) * rows].astype(dq_ref.dtype)


def run_tiles(pays, k, v, sums, heads, scale, kind):
    count = len(pays)
    n, pay_rows, _ = pays[0].shape
    rows, width = k.shape
    whole = pl.BlockSpec((rows, width), lambda i: (0, 0))
    pay_spec = pl.BlockSpec((1, pay_rows, LANES), lambda i: (i, 0, 0))
    dq_spec = pl.BlockSpec((1, width, rows), lambda i: (i, 0, 0))
    done = pl.pallas_call(
        functools.partial(tiles_kernel, count, heads, scale),
        grid=(n,),
        in_specs=[pay_spec] * count + [whole] * 4,
        out_specs=[dq_spec] * count + [whole] * 2,
        out_shape=[jax.ShapeDtypeStruct((n, width, rows), kind)] * count + [jax.ShapeDtypeStruct((rows, width), F32)] * 2,
        scratch_shapes=[pltpu.VMEM((width, rows), BF16)],
        input_output_aliases={count + 2: count, count + 3: count + 1},
        compiler_params=pltpu.CompilerParams(vmem_limit_bytes=VMEM_BYTES),
        cost_estimate=pl.CostEstimate(
            flops=40 * n * count * rows * rows * width // 2,
            bytes_accessed=n * count * (pay_rows * LANES * 2 + rows * width * 2),
            transcendentals=n * count * heads * rows * rows,
        ),
        name="tiles",
    )(*pays, k, v, *sums)
    return done[:count], tuple(done[count:])


def local(queries, key_vectors, value_vectors, forward_out, cotangent, log_norm):
    rows, width = queries.shape[3:]
    heads = log_norm.shape[3]
    scale = (width // heads) ** (-0.5)
    flat = (rows, width)
    k = key_vectors.reshape(flat)
    v = value_vectors.reshape(flat)
    own = make_payload(
        queries.reshape(flat), cotangent.reshape(flat), forward_out.reshape(flat), log_norm.reshape(heads, rows)
    )[None]
    sums = (jnp.zeros(flat, F32), jnp.zeros(flat, F32))
    work = functools.partial(run_tiles, k=k, v=v, heads=heads, scale=scale)

    def both(x, axis):
        return shift(x, axis, 1), shift(x, axis, -1)

    cols = both(own, "col")
    (dq_own,), sums = work([own], sums=sums, kind=F32)
    three = jnp.concatenate([own, *cols], axis=0)
    rows3 = both(three, "row")
    dq_cols, sums = work(cols, sums=sums, kind=F32)
    nine = jnp.concatenate([three, *rows3], axis=0)
    frames9 = both(nine, "frame")
    dq_rows, sums = work(rows3, sums=sums, kind=F32)
    dq_frames, sums = work(frames9, sums=sums, kind=BF16)

    from_next = shift(dq_frames[0], "frame", -1).astype(F32)
    from_prev = shift(dq_frames[1], "frame", 1).astype(F32)
    back = from_next + from_prev
    up = (dq_rows[0] + back[3:6]).astype(BF16)
    down = (dq_rows[1] + back[6:9]).astype(BF16)
    back3 = back[0:3] + shift(up, "row", -1).astype(F32) + shift(down, "row", 1).astype(F32)
    left = (dq_cols[0] + back3[1:2]).astype(BF16)
    right = (dq_cols[1] + back3[2:3]).astype(BF16)
    dq = dq_own + back3[0:1] + shift(left, "col", -1).astype(F32) + shift(right, "col", 1).astype(F32)

    dk, dv = sums
    out = queries.shape
    return (
        (dq[0].T * scale).astype(BF16).reshape(out),
        (dk * scale).astype(BF16).reshape(out),
        dv.astype(BF16).reshape(out),
    )


def solution(mesh):
    placed = P("frame", "row", "col", None, None)
    return jax.shard_map(
        local,
        mesh=mesh,
        in_specs=(placed,) * 6,
        out_specs=(placed,) * 3,
        check_vma=False,
    )
```

```python
import functools

import jax
import jax.numpy as jnp
from jax import lax
from jax.experimental import pallas as pl
from jax.experimental.pallas import tpu as pltpu
from jax.sharding import PartitionSpec as P

F32 = jnp.float32
BF16 = jnp.bfloat16
NT = (((1,), (1,)), ((), ()))
NN = (((1,), (0,)), ((), ()))
LANES = 128
VMEM_BYTES = 36 * 2**20


def dot(a, b, dims=NN):
    return lax.dot_general(a, b, dims, preferred_element_type=F32)


def meet(x, axis, second):
    pairs = []
    for i in range(second, lax.axis_size(axis) - 1, 2):
        pairs += [(i, i + 1), (i + 1, i)]
    return lax.ppermute(x, axis, pairs)


def payload_kernel(heads, q_ref, do_ref, o_ref, log_ref, k_ref, v_ref, pay_ref, kv_ref):
    rows = q_ref.shape[0]
    blocks = rows // LANES
    kv_ref[0] = k_ref[...]
    kv_ref[1] = v_ref[...]
    for h in range(heads):
        cols = slice(h * LANES, (h + 1) * LANES)
        pay_ref[0, h * rows:(h + 1) * rows, :] = q_ref[:, cols]
        pay_ref[0, (heads + h) * rows:(heads + h + 1) * rows, :] = do_ref[:, cols]
    products = do_ref[...].astype(F32) * o_ref[...].astype(F32)
    turned = products.T
    parts = []
    for h in range(heads):
        parts += [log_ref[h:h + 1, j * LANES:(j + 1) * LANES] for j in range(blocks)]
    for h in range(heads):
        delta = jnp.sum(turned[h * LANES:(h + 1) * LANES], axis=0, keepdims=True)
        parts += [delta[:, j * LANES:(j + 1) * LANES] for j in range(blocks)]
    parts.append(jnp.zeros((16 - len(parts), LANES), F32))
    rest = jnp.concatenate(parts, axis=0)
    at = 2 * heads * rows
    for piece in range(3):
        low = rest.astype(BF16)
        pay_ref[0, at + 16 * piece:at + 16 * (piece + 1), :] = low
        rest = rest - low.astype(F32)


def make_payloads(q, do, o, log_norm, k, v):
    rows, width = q.shape
    heads = log_norm.shape[0]
    return pl.pallas_call(
        functools.partial(payload_kernel, heads),
        out_shape=[
            jax.ShapeDtypeStruct((1, 2 * heads * rows + 48, LANES), BF16),
            jax.ShapeDtypeStruct((2, rows, width), BF16),
        ],
        compiler_params=pltpu.CompilerParams(vmem_limit_bytes=60 * 2**20),
        name="payloads",
    )(q, do, o, log_norm, k, v)


def tiles_kernel(count, sides, heads, scale, more_dq, more_acc, *refs):
    pays, refs = refs[:count], refs[count:]
    kvs, refs = refs[:sides], refs[sides:]
    dq_ins, refs = (refs[:count], refs[count:]) if more_dq else (None, refs)
    acc_ins, refs = (refs[:sides], refs[sides:]) if more_acc else (None, refs)
    dqs, refs = refs[:count], refs[count:]
    accs, kt_ref = refs[:sides], refs[sides]
    rows = kvs[0].shape[1]
    blocks = rows // LANES

    @pl.when(pl.program_id(0) == 0)
    def _():
        for s in range(sides):
            accs[s][...] = acc_ins[s][...] if more_acc else jnp.zeros_like(accs[s])
            kt_ref[:, s * rows:(s + 1) * rows] = kvs[s][0].astype(F32).T.astype(BF16)

    def row_of(aux, kind):
        return jnp.concatenate([aux[kind * blocks + j:kind * blocks + j + 1] for j in range(blocks)], axis=1)

    at = 2 * heads * rows
    auxes = []
    for pay in pays:
        aux = pay[0, at:, :].astype(F32)
        auxes.append(aux[0:16] + aux[16:32] + aux[32:48])
    for h in range(heads):
        cols = slice(h * LANES, (h + 1) * LANES)
        q = jnp.concatenate([pay[0, h * rows:(h + 1) * rows, :] for pay in pays], axis=0)
        do = jnp.concatenate([pay[0, (heads + h) * rows:(heads + h + 1) * rows, :] for pay in pays], axis=0)
        log = jnp.concatenate([row_of(aux, h) for aux in auxes], axis=1)
        delta = jnp.concatenate([row_of(aux, heads + h) for aux in auxes], axis=1)
        dq = None
        for s in range(sides):
            k = kvs[s][0, :, cols]
            v = kvs[s][1, :, cols]
            p = jnp.exp(dot(k, q, NT) * scale - log)
            ds = (p * (dot(v, do, NT) - delta)).astype(BF16)
            accs[s][1, :, cols] += dot(p.astype(BF16), do)
            accs[s][0, :, cols] += dot(ds, q)
            part = dot(kt_ref[cols, s * rows:(s + 1) * rows], ds)
            dq = part if dq is None else dq + part
        for i in range(count):
            mine = dq[:, i * rows:(i + 1) * rows]
            if more_dq:
                mine = mine + dq_ins[i][0, cols, :]
            dqs[i][0, cols, :] = mine.astype(dqs[i].dtype)


def run_tiles(pays, kvs, heads, scale, kinds, acc_kind=F32, dq_in=(), acc_in=()):
    count, sides = len(pays), len(kvs)
    n, pay_rows, _ = pays[0].shape
    _, rows, width = kvs[0].shape
    whole = pl.BlockSpec((2, rows, width), lambda i: (0, 0, 0))
    pay_spec = pl.BlockSpec((1, pay_rows, LANES), lambda i: (i, 0, 0))
    dq_spec = pl.BlockSpec((1, width, rows), lambda i: (i, 0, 0))
    done = pl.pallas_call(
        functools.partial(tiles_kernel, count, sides, heads, scale, bool(dq_in), bool(acc_in)),
        grid=(n,),
        in_specs=[pay_spec] * count + [whole] * sides + [dq_spec] * len(dq_in) + [whole] * len(acc_in),
        out_specs=[dq_spec] * count + [whole] * sides,
        out_shape=[jax.ShapeDtypeStruct((n, width, rows), kind) for kind in kinds]
        + [jax.ShapeDtypeStruct((2, rows, width), F32)] * sides,
        scratch_shapes=[pltpu.VMEM((width, sides * rows), BF16)],
        compiler_params=pltpu.CompilerParams(vmem_limit_bytes=VMEM_BYTES),
        cost_estimate=pl.CostEstimate(
            flops=20 * n * count * sides * rows * rows * width,
            bytes_accessed=n * count * (pay_rows * LANES * 2 + rows * width * 2),
            transcendentals=n * count * sides * heads * rows * rows,
        ),
        name="tiles",
    )(*pays, *kvs, *dq_in, *acc_in)
    return done[:count], done[count:]


def local(queries, key_vectors, value_vectors, forward_out, cotangent, log_norm):
    rows, width = queries.shape[3:]
    heads = log_norm.shape[3]
    scale = (width // heads) ** (-0.5)
    flat = (rows, width)
    own, own_kv = make_payloads(
        queries.reshape(flat),
        cotangent.reshape(flat),
        forward_out.reshape(flat),
        log_norm.reshape(heads, rows),
        key_vectors.reshape(flat),
        value_vectors.reshape(flat),
    )

    kv_b = meet(own_kv, "col", 1)
    kv_a = meet(own_kv, "col", 0)
    row_b = meet(own, "row", 1)
    row_a = meet(own, "row", 0)
    frame_b = meet(own, "frame", 1)
    frame_a = meet(own, "frame", 0)
    pair = jnp.concatenate([row_a, row_b], axis=0)
    pair_b = meet(pair, "frame", 1)
    pair_a = meet(pair, "frame", 0)

    work = functools.partial(run_tiles, heads=heads, scale=scale)
    near = [own, row_a, row_b, frame_a, frame_b]
    dqs, (acc_own,) = work(near, [own_kv], kinds=[F32] * 5)
    dqs, acc_ab = work(near, [kv_a, kv_b], dq_in=dqs, kinds=[F32] * 3 + [BF16] * 2)
    dq_own, dq_row_a, dq_row_b, dq_frame_a, dq_frame_b = dqs
    far_dqs, accs = work(
        [pair_a, pair_b], [own_kv, kv_a, kv_b], acc_in=(acc_own, *acc_ab), kinds=[BF16] * 2
    )

    own_back_b = meet(dq_frame_b, "frame", 1).astype(F32)
    own_back_a = meet(dq_frame_a, "frame", 0).astype(F32)
    pair_back = meet(far_dqs[1], "frame", 1).astype(F32) + meet(far_dqs[0], "frame", 0).astype(F32)
    dkv_b = meet(accs[2].astype(BF16), "col", 1).astype(F32)
    dkv_a = meet(accs[1].astype(BF16), "col", 0).astype(F32)
    row_back_b = meet((dq_row_b + pair_back[1:2]).astype(BF16), "row", 1).astype(F32)
    row_back_a = meet((dq_row_a + pair_back[0:1]).astype(BF16), "row", 0).astype(F32)
    dq = dq_own + own_back_a + own_back_b + row_back_a + row_back_b
    dkv = accs[0] + dkv_a + dkv_b

    out = queries.shape
    return (
        (dq[0].T * scale).astype(BF16).reshape(out),
        (dkv[0] * scale).astype(BF16).reshape(out),
        dkv[1].astype(BF16).reshape(out),
    )


def solution(mesh):
    placed = P("frame", "row", "col", None, None)
    return jax.shard_map(
        local,
        mesh=mesh,
        in_specs=(placed,) * 6,
        out_specs=(placed,) * 3,
        check_vma=False,
    )
```

```python
import functools

import jax
import jax.numpy as jnp
from jax import lax
from jax.experimental import pallas as pl
from jax.experimental.pallas import tpu as pltpu
from jax.sharding import PartitionSpec as P

F32 = jnp.float32
BF16 = jnp.bfloat16
NT = (((1,), (1,)), ((), ()))
NN = (((1,), (0,)), ((), ()))
LANES = 128
VMEM_BYTES = 36 * 2**20


def dot(a, b, dims=NN):
    return lax.dot_general(a, b, dims, preferred_element_type=F32)


def meet(x, axis, second):
    pairs = []
    for i in range(second, lax.axis_size(axis) - 1, 2):
        pairs += [(i, i + 1), (i + 1, i)]
    return lax.ppermute(x, axis, pairs)


def payload_kernel(heads, q_ref, do_ref, o_ref, log_ref, k_ref, v_ref, pay_ref, kv_ref):
    rows = q_ref.shape[0]
    blocks = rows // LANES
    kv_ref[0] = k_ref[...]
    kv_ref[1] = v_ref[...]
    for h in range(heads):
        cols = slice(h * LANES, (h + 1) * LANES)
        pay_ref[0, h * rows:(h + 1) * rows, :] = q_ref[:, cols]
        pay_ref[0, (heads + h) * rows:(heads + h + 1) * rows, :] = do_ref[:, cols]
    products = do_ref[...].astype(F32) * o_ref[...].astype(F32)
    turned = products.T
    parts = []
    for h in range(heads):
        parts += [log_ref[h:h + 1, j * LANES:(j + 1) * LANES] for j in range(blocks)]
    for h in range(heads):
        delta = jnp.sum(turned[h * LANES:(h + 1) * LANES], axis=0, keepdims=True)
        parts += [delta[:, j * LANES:(j + 1) * LANES] for j in range(blocks)]
    parts.append(jnp.zeros((16 - len(parts), LANES), F32))
    rest = jnp.concatenate(parts, axis=0)
    at = 2 * heads * rows
    for piece in range(3):
        low = rest.astype(BF16)
        pay_ref[0, at + 16 * piece:at + 16 * (piece + 1), :] = low
        rest = rest - low.astype(F32)


def make_payloads(q, do, o, log_norm, k, v):
    rows, width = q.shape
    heads = log_norm.shape[0]
    return pl.pallas_call(
        functools.partial(payload_kernel, heads),
        out_shape=[
            jax.ShapeDtypeStruct((1, 2 * heads * rows + 48, LANES), BF16),
            jax.ShapeDtypeStruct((2, rows, width), BF16),
        ],
        compiler_params=pltpu.CompilerParams(vmem_limit_bytes=60 * 2**20),
        name="payloads",
    )(q, do, o, log_norm, k, v)


def tiles_kernel(sizes, sides, heads, scale, dq_sizes, more_acc, groups, *refs):
    pay_refs, refs = refs[:len(sizes)], refs[len(sizes):]
    kvs, refs = refs[:sides], refs[sides:]
    dq_in_refs, refs = refs[:len(dq_sizes)], refs[len(dq_sizes):]
    acc_ins, refs = (refs[:sides], refs[sides:]) if more_acc else (None, refs)
    dqs, accs = refs[:len(groups)], refs[len(groups):]
    pays = [(ref, i) for ref, n in zip(pay_refs, sizes) for i in range(n)]
    dq_ins = [(ref, i) for ref, n in zip(dq_in_refs, dq_sizes) for i in range(n)]
    rows = kvs[0].shape[1]
    blocks = rows // LANES

    def row_of(aux, kind):
        return jnp.concatenate([aux[kind * blocks + j:kind * blocks + j + 1] for j in range(blocks)], axis=1)

    at = 2 * heads * rows
    auxes = []
    for ref, i in pays:
        aux = ref[i, at:, :].astype(F32)
        auxes.append(aux[0:16] + aux[16:32] + aux[32:48])
    for h in range(heads):
        cols = slice(h * LANES, (h + 1) * LANES)
        q = jnp.concatenate([ref[i, h * rows:(h + 1) * rows, :] for ref, i in pays], axis=0)
        do = jnp.concatenate([ref[i, (heads + h) * rows:(heads + h + 1) * rows, :] for ref, i in pays], axis=0)
        log = jnp.concatenate([row_of(aux, h) for aux in auxes], axis=1)
        delta = jnp.concatenate([row_of(aux, heads + h) for aux in auxes], axis=1)
        dq = None
        for s in range(sides):
            k = kvs[s][0, :, cols]
            v = kvs[s][1, :, cols]
            p = jnp.exp(dot(k, q, NT) * scale - log)
            ds = (p * (dot(v, do, NT) - delta)).astype(BF16)
            dv = dot(p.astype(BF16), do)
            dk = dot(ds, q)
            if more_acc:
                dv = dv + acc_ins[s][1, :, cols]
                dk = dk + acc_ins[s][0, :, cols]
            accs[s][1, :, cols] = dv.astype(accs[s].dtype)
            accs[s][0, :, cols] = dk.astype(accs[s].dtype)
            part = dot(k.astype(F32).T.astype(BF16), ds)
            dq = part if dq is None else dq + part
        for out, group in zip(dqs, groups):
            for at_out, tile in enumerate(group):
                mine = dq[:, tile * rows:(tile + 1) * rows]
                if dq_ins:
                    ref, i = dq_ins[tile]
                    mine = mine + ref[i, cols, :]
                out[at_out, cols, :] = mine.astype(out.dtype)


def run_tiles(pays, kvs, heads, scale, groups, kinds, acc_kinds, dq_in=(), acc_in=(), weight=1):
    sizes = [pay.shape[0] for pay in pays]
    _, rows, width = kvs[0].shape
    here = pl.BlockSpec(memory_space=pltpu.VMEM)
    done = pl.pallas_call(
        functools.partial(
            tiles_kernel, sizes, len(kvs), heads, scale, [x.shape[0] for x in dq_in], bool(acc_in), groups
        ),
        in_specs=[here] * (len(pays) + len(kvs) + len(dq_in) + len(acc_in)),
        out_specs=[here] * (len(groups) + len(kvs)),
        out_shape=[jax.ShapeDtypeStruct((len(group), width, rows), kind) for group, kind in zip(groups, kinds)]
        + [jax.ShapeDtypeStruct((2, rows, width), kind) for kind in acc_kinds],
        compiler_params=pltpu.CompilerParams(vmem_limit_bytes=VMEM_BYTES),
        cost_estimate=pl.CostEstimate(
            flops=weight * 10 * sum(sizes) * len(kvs) * rows * rows * width, bytes_accessed=0, transcendentals=0
        ),
        name="tiles",
    )(*pays, *kvs, *dq_in, *acc_in)
    return done[:len(groups)], done[len(groups):]


def finish_kernel(scale, dq_ref, a_ref, b_ref, row_a_ref, row_b_ref, dkv_ref, dkv_a_ref, dkv_b_ref, q_out, k_out, v_out):
    dkv = [dkv_ref[i] + dkv_a_ref[i].astype(F32) + dkv_b_ref[i].astype(F32) for i in range(2)]
    k_out[...] = (dkv[0] * scale).astype(BF16)
    v_out[...] = dkv[1].astype(BF16)
    dq = dq_ref[0]
    for ref in (a_ref, b_ref, row_a_ref, row_b_ref):
        dq = dq + ref[0].astype(F32)
    q_out[...] = (dq * scale).T.astype(BF16)


def finish(dq, a, b, row_a, row_b, dkv, dkv_a, dkv_b, scale):
    _, rows, width = dkv.shape
    return pl.pallas_call(
        functools.partial(finish_kernel, scale),
        out_shape=[jax.ShapeDtypeStruct((rows, width), BF16)] * 3,
        compiler_params=pltpu.CompilerParams(vmem_limit_bytes=VMEM_BYTES),
        name="finish",
    )(dq, a, b, row_a, row_b, dkv, dkv_a, dkv_b)


def local(queries, key_vectors, value_vectors, forward_out, cotangent, log_norm):
    rows, width = queries.shape[3:]
    heads = log_norm.shape[3]
    scale = (width // heads) ** (-0.5)
    flat = (rows, width)
    own, own_kv = make_payloads(
        queries.reshape(flat),
        cotangent.reshape(flat),
        forward_out.reshape(flat),
        log_norm.reshape(heads, rows),
        key_vectors.reshape(flat),
        value_vectors.reshape(flat),
    )

    kv_b = meet(own_kv, "col", 1)
    kv_a = meet(own_kv, "col", 0)
    row_b = meet(own, "row", 1)
    row_a = meet(own, "row", 0)
    frame_b = meet(own, "frame", 1)
    frame_a = meet(own, "frame", 0)
    pair = jnp.concatenate([row_a, row_b], axis=0)
    pair_b = meet(pair, "frame", 1)
    pair_a = meet(pair, "frame", 0)

    work = functools.partial(run_tiles, heads=heads, scale=scale)
    near = [own, row_a, row_b, frame_a, frame_b]
    far = [pair_a, pair_b]
    near_dqs, accs = work(
        near, [own_kv, kv_a], groups=[[0], [1], [2], [3], [4]], kinds=[F32] * 5, acc_kinds=[F32] * 2, weight=3
    )
    far_dqs, (dkv, to_a) = work(
        far, [own_kv, kv_a], acc_in=accs, groups=[[0, 1], [2, 3]], kinds=[F32] * 2, acc_kinds=[F32, BF16], weight=0
    )
    (dq_own, dq_row_a, dq_row_b, dq_frame_a, dq_frame_b), (to_b,) = work(
        near + far,
        [kv_b],
        dq_in=[*near_dqs, *far_dqs],
        groups=[[0], [1], [2], [3, 5, 6], [4, 7, 8]],
        kinds=[F32] * 3 + [BF16] * 2,
        acc_kinds=[BF16],
        weight=0,
    )

    dkv_b = meet(to_b, "col", 1)
    dkv_a = meet(to_a, "col", 0)
    back_b = meet(dq_frame_b, "frame", 1)
    back_a = meet(dq_frame_a, "frame", 0)
    back = back_b.astype(F32) + back_a.astype(F32)
    row_back_b = meet((dq_row_b + back[2:3]).astype(BF16), "row", 1)
    row_back_a = meet((dq_row_a + back[1:2]).astype(BF16), "row", 0)
    grads = finish(dq_own, back_a, back_b, row_back_a, row_back_b, dkv, dkv_a, dkv_b, scale)
    return tuple(grad.reshape(queries.shape) for grad in grads)


def solution(mesh):
    placed = P("frame", "row", "col", None, None)
    return jax.shard_map(
        local,
        mesh=mesh,
        in_specs=(placed,) * 6,
        out_specs=(placed,) * 3,
        check_vma=False,
    )
```

```python
import functools

import jax
import jax.numpy as jnp
from jax import lax
from jax.experimental import pallas as pl
from jax.experimental.pallas import tpu as pltpu
from jax.sharding import PartitionSpec as P

F32 = jnp.float32
BF16 = jnp.bfloat16
NT = (((1,), (1,)), ((), ()))
NN = (((1,), (0,)), ((), ()))
LANES = 128
CHUNK = 256
LOG2_E = 1.4426950408889634
VMEM_BYTES = 36 * 2**20


def dot(a, b, dims=NN):
    return lax.dot_general(a, b, dims, preferred_element_type=F32)


def meet(x, axis, second):
    pairs = []
    for i in range(second, lax.axis_size(axis) - 1, 2):
        pairs += [(i, i + 1), (i + 1, i)]
    return lax.ppermute(x, axis, pairs)


def payload_kernel(heads, q_ref, do_ref, o_ref, log_ref, k_ref, v_ref, pay_ref, kv_ref, o_buf, log_buf, sems):
    rows = q_ref.shape[0]
    blocks = rows // LANES
    copies = []

    def copy(src, dst):
        copies.append(pltpu.make_async_copy(src, dst, sems.at[len(copies)]))
        copies[-1].start()

    for h in range(heads):
        copy(do_ref.at[:, h * LANES:(h + 1) * LANES], pay_ref.at[0, (heads + h) * rows:(heads + h + 1) * rows, :])
    copy(o_ref, o_buf)
    copy(log_ref, log_buf)
    needed = len(copies)
    for h in range(heads):
        copy(q_ref.at[:, h * LANES:(h + 1) * LANES], pay_ref.at[0, h * rows:(h + 1) * rows, :])
    copy(k_ref, kv_ref.at[0])
    copy(v_ref, kv_ref.at[1])
    for one in copies[:needed]:
        one.wait()
    parts = []
    for h in range(heads):
        parts += [log_buf[h:h + 1, j * LANES:(j + 1) * LANES] for j in range(blocks)]
    for h in range(heads):
        do = pay_ref[0, (heads + h) * rows:(heads + h + 1) * rows, :].astype(F32)
        products = do * o_buf[:, h * LANES:(h + 1) * LANES].astype(F32)
        delta = jnp.sum(products.T, axis=0, keepdims=True)
        parts += [delta[:, j * LANES:(j + 1) * LANES] for j in range(blocks)]
    parts.append(jnp.zeros((16 - len(parts), LANES), F32))
    rest = jnp.concatenate(parts, axis=0)
    at = 2 * heads * rows
    for piece in range(3):
        low = rest.astype(BF16)
        pay_ref[0, at + 16 * piece:at + 16 * (piece + 1), :] = low
        rest = rest - low.astype(F32)
    for one in copies[needed:]:
        one.wait()


def make_payloads(q, do, o, log_norm, k, v):
    rows, width = q.shape
    heads = log_norm.shape[0]
    return pl.pallas_call(
        functools.partial(payload_kernel, heads),
        in_specs=[pl.BlockSpec(memory_space=pltpu.HBM)] * 6,
        out_specs=[pl.BlockSpec(memory_space=pltpu.VMEM)] * 2,
        out_shape=[
            jax.ShapeDtypeStruct((1, 2 * heads * rows + 48, LANES), BF16),
            jax.ShapeDtypeStruct((2, rows, width), BF16),
        ],
        scratch_shapes=[
            pltpu.VMEM((rows, width), BF16),
            pltpu.VMEM(log_norm.shape, F32),
            pltpu.SemaphoreType.DMA((2 * heads + 4,)),
        ],
        compiler_params=pltpu.CompilerParams(vmem_limit_bytes=60 * 2**20),
        name="payloads",
    )(q, do, o, log_norm, k, v)


def tiles_kernel(sizes, sides, heads, scale, dq_sizes, more_acc, groups, *refs):
    pay_refs, refs = refs[:len(sizes)], refs[len(sizes):]
    kvs, refs = refs[:sides], refs[sides:]
    dq_in_refs, refs = refs[:len(dq_sizes)], refs[len(dq_sizes):]
    acc_ins, refs = (refs[:sides], refs[sides:]) if more_acc else (None, refs)
    dqs, refs = refs[:len(groups)], refs[len(groups):]
    accs, (p_ref, ds_ref) = refs[:sides], refs[sides:]
    pays = [(ref, i) for ref, n in zip(pay_refs, sizes) for i in range(n)]
    dq_ins = [(ref, i) for ref, n in zip(dq_in_refs, dq_sizes) for i in range(n)]
    rows = kvs[0].shape[1]
    blocks = rows // LANES

    def row_of(aux, kind):
        return jnp.concatenate([aux[kind * blocks + j:kind * blocks + j + 1] for j in range(blocks)], axis=1)

    at = 2 * heads * rows
    auxes = []
    for ref, i in pays:
        aux = ref[i, at:, :].astype(F32)
        auxes.append(aux[0:16] + aux[16:32] + aux[32:48])
    for h in range(heads):
        cols = slice(h * LANES, (h + 1) * LANES)
        q = jnp.concatenate([ref[i, h * rows:(h + 1) * rows, :] for ref, i in pays], axis=0)
        do = jnp.concatenate([ref[i, (heads + h) * rows:(heads + h + 1) * rows, :] for ref, i in pays], axis=0)
        log = jnp.concatenate([row_of(aux, h) for aux in auxes], axis=1)
        delta = jnp.concatenate([row_of(aux, heads + h) for aux in auxes], axis=1)
        log = log * LOG2_E
        dq = None
        for s in range(sides):
            k = kvs[s][0, :, cols]
            v = kvs[s][1, :, cols]
            for start in range(0, q.shape[0], CHUNK):
                part = slice(start, min(start + CHUNK, q.shape[0]))
                p = jnp.exp2(dot(k, q[part], NT) * (scale * LOG2_E) - log[:, part])
                ds = p * (dot(v, do[part], NT) - delta[:, part])
                p_ref[h * sides + s, :, part] = p.astype(BF16)
                ds_ref[h * sides + s, :, part] = ds.astype(BF16)
            p = p_ref[h * sides + s]
            ds = ds_ref[h * sides + s]
            dv = dot(p, do)
            dk = dot(ds, q)
            if more_acc:
                dv = dv + acc_ins[s][1, :, cols]
                dk = dk + acc_ins[s][0, :, cols]
            accs[s][1, :, cols] = dv.astype(accs[s].dtype)
            accs[s][0, :, cols] = dk.astype(accs[s].dtype)
            part = dot(k.astype(F32).T.astype(BF16), ds)
            dq = part if dq is None else dq + part
        for out, group in zip(dqs, groups):
            for at_out, tile in enumerate(group):
                mine = dq[:, tile * rows:(tile + 1) * rows]
                if dq_ins:
                    ref, i = dq_ins[tile]
                    mine = mine + ref[i, cols, :]
                out[at_out, cols, :] = mine.astype(out.dtype)


def run_tiles(pays, kvs, heads, scale, groups, kinds, acc_kinds, dq_in=(), acc_in=(), weight=1):
    sizes = [pay.shape[0] for pay in pays]
    _, rows, width = kvs[0].shape
    here = pl.BlockSpec(memory_space=pltpu.VMEM)
    done = pl.pallas_call(
        functools.partial(
            tiles_kernel, sizes, len(kvs), heads, scale, [x.shape[0] for x in dq_in], bool(acc_in), groups
        ),
        in_specs=[here] * (len(pays) + len(kvs) + len(dq_in) + len(acc_in)),
        out_specs=[here] * (len(groups) + len(kvs)),
        out_shape=[jax.ShapeDtypeStruct((len(group), width, rows), kind) for group, kind in zip(groups, kinds)]
        + [jax.ShapeDtypeStruct((2, rows, width), kind) for kind in acc_kinds],
        scratch_shapes=[pltpu.VMEM((heads * len(kvs), rows, sum(sizes) * rows), BF16)] * 2,
        compiler_params=pltpu.CompilerParams(vmem_limit_bytes=VMEM_BYTES),
        cost_estimate=pl.CostEstimate(
            flops=weight * 10 * sum(sizes) * len(kvs) * rows * rows * width, bytes_accessed=0, transcendentals=0
        ),
        name="tiles",
    )(*pays, *kvs, *dq_in, *acc_in)
    return done[:len(groups)], done[len(groups):]


def finish_kernel(scale, dq_ref, a_ref, b_ref, row_a_ref, row_b_ref, dkv_ref, dkv_a_ref, dkv_b_ref, q_out, k_out, v_out):
    dkv = [dkv_ref[i] + dkv_a_ref[i].astype(F32) + dkv_b_ref[i].astype(F32) for i in range(2)]
    k_out[...] = (dkv[0] * scale).astype(BF16)
    v_out[...] = dkv[1].astype(BF16)
    dq = dq_ref[0]
    for ref in (a_ref, b_ref, row_a_ref, row_b_ref):
        dq = dq + ref[0].astype(F32)
    q_out[...] = (dq * scale).T.astype(BF16)


def finish(dq, a, b, row_a, row_b, dkv, dkv_a, dkv_b, scale):
    _, rows, width = dkv.shape
    return pl.pallas_call(
        functools.partial(finish_kernel, scale),
        out_shape=[jax.ShapeDtypeStruct((rows, width), BF16)] * 3,
        compiler_params=pltpu.CompilerParams(vmem_limit_bytes=VMEM_BYTES),
        name="finish",
    )(dq, a, b, row_a, row_b, dkv, dkv_a, dkv_b)


def local(queries, key_vectors, value_vectors, forward_out, cotangent, log_norm):
    rows, width = queries.shape[3:]
    heads = log_norm.shape[3]
    scale = (width // heads) ** (-0.5)
    flat = (rows, width)
    own, own_kv = make_payloads(
        queries.reshape(flat),
        cotangent.reshape(flat),
        forward_out.reshape(flat),
        log_norm.reshape(heads, rows),
        key_vectors.reshape(flat),
        value_vectors.reshape(flat),
    )

    kv_b = meet(own_kv, "col", 1)
    kv_a = meet(own_kv, "col", 0)
    row_b = meet(own, "row", 1)
    row_a = meet(own, "row", 0)
    frame_b = meet(own, "frame", 1)
    frame_a = meet(own, "frame", 0)
    pair = jnp.concatenate([row_a, row_b], axis=0)
    pair_b = meet(pair, "frame", 1)
    pair_a = meet(pair, "frame", 0)

    work = functools.partial(run_tiles, heads=heads, scale=scale)
    near = [own, row_a, row_b, frame_a, frame_b]
    far = [pair_a, pair_b]
    near_dqs, accs = work(
        near, [own_kv, kv_a], groups=[[0], [1], [2], [3], [4]], kinds=[F32] * 5, acc_kinds=[F32] * 2, weight=3
    )
    far_dqs, (dkv, to_a) = work(
        far, [own_kv, kv_a], acc_in=accs, groups=[[0, 1], [2, 3]], kinds=[F32] * 2, acc_kinds=[F32, BF16], weight=0
    )
    (dq_own, dq_row_a, dq_row_b, dq_frame_a, dq_frame_b), (to_b,) = work(
        near + far,
        [kv_b],
        dq_in=[*near_dqs, *far_dqs],
        groups=[[0], [1], [2], [3, 5, 6], [4, 7, 8]],
        kinds=[F32] * 3 + [BF16] * 2,
        acc_kinds=[BF16],
        weight=0,
    )

    dkv_b = meet(to_b, "col", 1)
    dkv_a = meet(to_a, "col", 0)
    back_b = meet(dq_frame_b, "frame", 1)
    back_a = meet(dq_frame_a, "frame", 0)
    back = back_b.astype(F32) + back_a.astype(F32)
    row_back_b = meet((dq_row_b + back[2:3]).astype(BF16), "row", 1)
    row_back_a = meet((dq_row_a + back[1:2]).astype(BF16), "row", 0)
    grads = finish(dq_own, back_a, back_b, row_back_a, row_back_b, dkv, dkv_a, dkv_b, scale)
    return tuple(grad.reshape(queries.shape) for grad in grads)


def solution(mesh):
    placed = P("frame", "row", "col", None, None)
    return jax.shard_map(
        local,
        mesh=mesh,
        in_specs=(placed,) * 6,
        out_specs=(placed,) * 3,
        check_vma=False,
    )
```

```python
import functools

import jax
import jax.numpy as jnp
from jax import lax
from jax.experimental import pallas as pl
from jax.experimental.pallas import tpu as pltpu
from jax.sharding import PartitionSpec as P

F32 = jnp.float32
BF16 = jnp.bfloat16
NT = (((1,), (1,)), ((), ()))
NN = (((1,), (0,)), ((), ()))
LANES = 128
CHUNK = 256
LOG2_E = 1.4426950408889634
VMEM_BYTES = 36 * 2**20


def dot(a, b, dims=NN):
    return lax.dot_general(a, b, dims, preferred_element_type=F32)


def meet(x, axis, second):
    pairs = []
    for i in range(second, lax.axis_size(axis) - 1, 2):
        pairs += [(i, i + 1), (i + 1, i)]
    return lax.ppermute(x, axis, pairs)


def payload_kernel(heads, q_ref, do_ref, o_ref, log_ref, k_ref, v_ref, pay_ref, kv_ref, o_buf, log_buf, sems):
    rows = q_ref.shape[0]
    blocks = rows // LANES
    copies = []

    def copy(src, dst):
        copies.append(pltpu.make_async_copy(src, dst, sems.at[len(copies)]))
        copies[-1].start()

    for h in range(heads):
        copy(do_ref.at[:, h * LANES:(h + 1) * LANES], pay_ref.at[0, (heads + h) * rows:(heads + h + 1) * rows, :])
    copy(o_ref, o_buf)
    copy(log_ref, log_buf)
    needed = len(copies)
    for h in range(heads):
        copy(q_ref.at[:, h * LANES:(h + 1) * LANES], pay_ref.at[0, h * rows:(h + 1) * rows, :])
    copy(k_ref, kv_ref.at[0])
    copy(v_ref, kv_ref.at[1])
    for one in copies[:needed]:
        one.wait()
    parts = []
    for h in range(heads):
        parts += [log_buf[h:h + 1, j * LANES:(j + 1) * LANES] for j in range(blocks)]
    for h in range(heads):
        do = pay_ref[0, (heads + h) * rows:(heads + h + 1) * rows, :].astype(F32)
        products = do * o_buf[:, h * LANES:(h + 1) * LANES].astype(F32)
        delta = jnp.sum(products.T, axis=0, keepdims=True)
        parts += [delta[:, j * LANES:(j + 1) * LANES] for j in range(blocks)]
    parts.append(jnp.zeros((16 - len(parts), LANES), F32))
    rest = jnp.concatenate(parts, axis=0)
    at = 2 * heads * rows
    for piece in range(3):
        low = rest.astype(BF16)
        pay_ref[0, at + 16 * piece:at + 16 * (piece + 1), :] = low
        rest = rest - low.astype(F32)
    for one in copies[needed:]:
        one.wait()


def make_payloads(q, do, o, log_norm, k, v):
    rows, width = q.shape
    heads = log_norm.shape[0]
    return pl.pallas_call(
        functools.partial(payload_kernel, heads),
        in_specs=[pl.BlockSpec(memory_space=pltpu.HBM)] * 6,
        out_specs=[pl.BlockSpec(memory_space=pltpu.VMEM)] * 2,
        out_shape=[
            jax.ShapeDtypeStruct((1, 2 * heads * rows + 48, LANES), BF16),
            jax.ShapeDtypeStruct((2, rows, width), BF16),
        ],
        scratch_shapes=[
            pltpu.VMEM((rows, width), BF16),
            pltpu.VMEM(log_norm.shape, F32),
            pltpu.SemaphoreType.DMA((2 * heads + 4,)),
        ],
        compiler_params=pltpu.CompilerParams(vmem_limit_bytes=60 * 2**20),
        name="payloads",
    )(q, do, o, log_norm, k, v)


def tiles_kernel(sizes, sides, heads, scale, dq_sizes, more_acc, groups, *refs):
    pay_refs, refs = refs[:len(sizes)], refs[len(sizes):]
    kvs, refs = refs[:sides], refs[sides:]
    dq_in_refs, refs = refs[:len(dq_sizes)], refs[len(dq_sizes):]
    acc_ins, refs = (refs[:sides], refs[sides:]) if more_acc else (None, refs)
    dqs, refs = refs[:len(groups)], refs[len(groups):]
    accs, (p_ref, ds_ref) = refs[:sides], refs[sides:]
    pays = [(ref, i) for ref, n in zip(pay_refs, sizes) for i in range(n)]
    dq_ins = [(ref, i) for ref, n in zip(dq_in_refs, dq_sizes) for i in range(n)]
    rows = kvs[0].shape[1]
    blocks = rows // LANES

    def row_of(aux, kind):
        return jnp.concatenate([aux[kind * blocks + j:kind * blocks + j + 1] for j in range(blocks)], axis=1)

    at = 2 * heads * rows
    auxes = []
    for ref, i in pays:
        aux = ref[i, at:, :].astype(F32)
        auxes.append(aux[0:16] + aux[16:32] + aux[32:48])
    for h in range(heads):
        cols = slice(h * LANES, (h + 1) * LANES)
        q = jnp.concatenate([ref[i, h * rows:(h + 1) * rows, :] for ref, i in pays], axis=0)
        do = jnp.concatenate([ref[i, (heads + h) * rows:(heads + h + 1) * rows, :] for ref, i in pays], axis=0)
        log = jnp.concatenate([row_of(aux, h) for aux in auxes], axis=1)
        delta = jnp.concatenate([row_of(aux, heads + h) for aux in auxes], axis=1)
        log = log * LOG2_E
        turned = []
        for s in range(sides):
            k = kvs[s][0, :, cols]
            v = kvs[s][1, :, cols]
            for start in range(0, q.shape[0], CHUNK):
                part = slice(start, min(start + CHUNK, q.shape[0]))
                p = jnp.exp2(dot(k, q[part], NT) * (scale * LOG2_E) - log[:, part])
                ds = p * (dot(v, do[part], NT) - delta[:, part])
                p_ref[h * sides + s, :, part] = p.astype(BF16)
                ds_ref[h * sides + s, :, part] = ds.astype(BF16)
            p = p_ref[h * sides + s]
            ds = ds_ref[h * sides + s]
            dv = dot(p, do)
            dk = dot(ds, q)
            if more_acc:
                dv = dv + acc_ins[s][1, :, cols]
                dk = dk + acc_ins[s][0, :, cols]
            accs[s][1, :, cols] = dv.astype(accs[s].dtype)
            accs[s][0, :, cols] = dk.astype(accs[s].dtype)
            turned.append(k.astype(F32).T.astype(BF16))
        all_ds = ds_ref[h * sides:(h + 1) * sides].reshape(sides * rows, q.shape[0])
        dq = dot(jnp.concatenate(turned, axis=1), all_ds)
        for out, group in zip(dqs, groups):
            for at_out, tile in enumerate(group):
                mine = dq[:, tile * rows:(tile + 1) * rows]
                if dq_ins:
                    ref, i = dq_ins[tile]
                    mine = mine + ref[i, cols, :]
                out[at_out, cols, :] = mine.astype(out.dtype)


def run_tiles(pays, kvs, heads, scale, groups, kinds, acc_kinds, dq_in=(), acc_in=(), weight=1):
    sizes = [pay.shape[0] for pay in pays]
    _, rows, width = kvs[0].shape
    here = pl.BlockSpec(memory_space=pltpu.VMEM)
    done = pl.pallas_call(
        functools.partial(
            tiles_kernel, sizes, len(kvs), heads, scale, [x.shape[0] for x in dq_in], bool(acc_in), groups
        ),
        in_specs=[here] * (len(pays) + len(kvs) + len(dq_in) + len(acc_in)),
        out_specs=[here] * (len(groups) + len(kvs)),
        out_shape=[jax.ShapeDtypeStruct((len(group), width, rows), kind) for group, kind in zip(groups, kinds)]
        + [jax.ShapeDtypeStruct((2, rows, width), kind) for kind in acc_kinds],
        scratch_shapes=[pltpu.VMEM((heads * len(kvs), rows, sum(sizes) * rows), BF16)] * 2,
        compiler_params=pltpu.CompilerParams(vmem_limit_bytes=VMEM_BYTES),
        cost_estimate=pl.CostEstimate(
            flops=weight * 10 * sum(sizes) * len(kvs) * rows * rows * width, bytes_accessed=0, transcendentals=0
        ),
        name="tiles",
    )(*pays, *kvs, *dq_in, *acc_in)
    return done[:len(groups)], done[len(groups):]


def finish_kernel(scale, dq_ref, a_ref, b_ref, row_a_ref, row_b_ref, dkv_ref, dkv_a_ref, dkv_b_ref, q_out, k_out, v_out):
    dkv = [dkv_ref[i] + dkv_a_ref[i].astype(F32) + dkv_b_ref[i].astype(F32) for i in range(2)]
    k_out[...] = (dkv[0] * scale).astype(BF16)
    v_out[...] = dkv[1].astype(BF16)
    dq = dq_ref[0]
    for ref in (a_ref, b_ref, row_a_ref, row_b_ref):
        dq = dq + ref[0].astype(F32)
    q_out[...] = (dq * scale).T.astype(BF16)


def finish(dq, a, b, row_a, row_b, dkv, dkv_a, dkv_b, scale):
    _, rows, width = dkv.shape
    return pl.pallas_call(
        functools.partial(finish_kernel, scale),
        out_shape=[jax.ShapeDtypeStruct((rows, width), BF16)] * 3,
        compiler_params=pltpu.CompilerParams(vmem_limit_bytes=VMEM_BYTES),
        name="finish",
    )(dq, a, b, row_a, row_b, dkv, dkv_a, dkv_b)


def local(queries, key_vectors, value_vectors, forward_out, cotangent, log_norm):
    rows, width = queries.shape[3:]
    heads = log_norm.shape[3]
    scale = (width // heads) ** (-0.5)
    flat = (rows, width)
    own, own_kv = make_payloads(
        queries.reshape(flat),
        cotangent.reshape(flat),
        forward_out.reshape(flat),
        log_norm.reshape(heads, rows),
        key_vectors.reshape(flat),
        value_vectors.reshape(flat),
    )

    kv_b = meet(own_kv, "col", 1)
    kv_a = meet(own_kv, "col", 0)
    row_b = meet(own, "row", 1)
    row_a = meet(own, "row", 0)
    frame_b = meet(own, "frame", 1)
    frame_a = meet(own, "frame", 0)
    pair = jnp.concatenate([row_a, row_b], axis=0)
    pair_b = meet(pair, "frame", 1)
    pair_a = meet(pair, "frame", 0)

    work = functools.partial(run_tiles, heads=heads, scale=scale)
    near = [own, row_a, row_b, frame_a, frame_b]
    far = [pair_a, pair_b]
    near_dqs, accs = work(
        near, [own_kv, kv_a], groups=[[0], [1], [2], [3], [4]], kinds=[F32] * 5, acc_kinds=[F32] * 2, weight=3
    )
    far_dqs, (dkv, to_a) = work(
        far, [own_kv, kv_a], acc_in=accs, groups=[[0, 1], [2, 3]], kinds=[F32] * 2, acc_kinds=[F32, BF16], weight=0
    )
    (dq_own, dq_row_a, dq_row_b, dq_frame_a, dq_frame_b), (to_b,) = work(
        near + far,
        [kv_b],
        dq_in=[*near_dqs, *far_dqs],
        groups=[[0], [1], [2], [3, 5, 6], [4, 7, 8]],
        kinds=[F32] * 3 + [BF16] * 2,
        acc_kinds=[BF16],
        weight=0,
    )

    dkv_b = meet(to_b, "col", 1)
    dkv_a = meet(to_a, "col", 0)
    back_b = meet(dq_frame_b, "frame", 1)
    back_a = meet(dq_frame_a, "frame", 0)
    back = back_b.astype(F32) + back_a.astype(F32)
    row_back_b = meet((dq_row_b + back[2:3]).astype(BF16), "row", 1)
    row_back_a = meet((dq_row_a + back[1:2]).astype(BF16), "row", 0)
    grads = finish(dq_own, back_a, back_b, row_back_a, row_back_b, dkv, dkv_a, dkv_b, scale)
    return tuple(grad.reshape(queries.shape) for grad in grads)


def solution(mesh):
    placed = P("frame", "row", "col", None, None)
    return jax.shard_map(
        local,
        mesh=mesh,
        in_specs=(placed,) * 6,
        out_specs=(placed,) * 3,
        check_vma=False,
    )
```

```python
import functools

import jax
import jax.numpy as jnp
from jax import lax
from jax.experimental import pallas as pl
from jax.experimental.pallas import tpu as pltpu
from jax.sharding import PartitionSpec as P

F32 = jnp.float32
BF16 = jnp.bfloat16
NT = (((1,), (1,)), ((), ()))
NN = (((1,), (0,)), ((), ()))
LANES = 128
CHUNK = 256
LOG2_E = 1.4426950408889634
VMEM_BYTES = 36 * 2**20


def dot(a, b, dims=NN):
    return lax.dot_general(a, b, dims, preferred_element_type=F32)


def meet(x, axis, second):
    pairs = []
    for i in range(second, lax.axis_size(axis) - 1, 2):
        pairs += [(i, i + 1), (i + 1, i)]
    return lax.ppermute(x, axis, pairs)


def payload_kernel(heads, q_ref, do_ref, o_ref, log_ref, k_ref, v_ref, pay_ref, kv_ref, o_buf, log_buf, sems):
    rows = q_ref.shape[0]
    blocks = rows // LANES
    copies = []

    def copy(src, dst):
        copies.append(pltpu.make_async_copy(src, dst, sems.at[len(copies)]))
        copies[-1].start()

    for h in range(heads):
        copy(do_ref.at[:, h * LANES:(h + 1) * LANES], pay_ref.at[0, (heads + h) * rows:(heads + h + 1) * rows, :])
    copy(o_ref, o_buf)
    copy(log_ref, log_buf)
    needed = len(copies)
    for h in range(heads):
        copy(q_ref.at[:, h * LANES:(h + 1) * LANES], pay_ref.at[0, h * rows:(h + 1) * rows, :])
    copy(k_ref, kv_ref.at[0])
    copy(v_ref, kv_ref.at[1])
    for one in copies[:needed]:
        one.wait()
    parts = []
    for h in range(heads):
        parts += [log_buf[h:h + 1, j * LANES:(j + 1) * LANES] for j in range(blocks)]
    for h in range(heads):
        do = pay_ref[0, (heads + h) * rows:(heads + h + 1) * rows, :].astype(F32)
        products = do * o_buf[:, h * LANES:(h + 1) * LANES].astype(F32)
        delta = jnp.sum(products.T, axis=0, keepdims=True)
        parts += [delta[:, j * LANES:(j + 1) * LANES] for j in range(blocks)]
    parts.append(jnp.zeros((16 - len(parts), LANES), F32))
    rest = jnp.concatenate(parts, axis=0)
    at = 2 * heads * rows
    for piece in range(3):
        low = rest.astype(BF16)
        pay_ref[0, at + 16 * piece:at + 16 * (piece + 1), :] = low
        rest = rest - low.astype(F32)
    for one in copies[needed:]:
        one.wait()


def make_payloads(q, do, o, log_norm, k, v):
    rows, width = q.shape
    heads = log_norm.shape[0]
    return pl.pallas_call(
        functools.partial(payload_kernel, heads),
        in_specs=[pl.BlockSpec(memory_space=pltpu.HBM)] * 6,
        out_specs=[pl.BlockSpec(memory_space=pltpu.VMEM)] * 2,
        out_shape=[
            jax.ShapeDtypeStruct((1, 2 * heads * rows + 48, LANES), BF16),
            jax.ShapeDtypeStruct((2, rows, width), BF16),
        ],
        scratch_shapes=[
            pltpu.VMEM((rows, width), BF16),
            pltpu.VMEM(log_norm.shape, F32),
            pltpu.SemaphoreType.DMA((2 * heads + 4,)),
        ],
        compiler_params=pltpu.CompilerParams(vmem_limit_bytes=60 * 2**20),
        name="payloads",
    )(q, do, o, log_norm, k, v)


def tiles_kernel(sizes, sides, heads, scale, dq_sizes, more_acc, groups, *refs):
    pay_refs, refs = refs[:len(sizes)], refs[len(sizes):]
    kvs, refs = refs[:sides], refs[sides:]
    dq_in_refs, refs = refs[:len(dq_sizes)], refs[len(dq_sizes):]
    acc_ins, refs = (refs[:sides], refs[sides:]) if more_acc else (None, refs)
    dqs, refs = refs[:len(groups)], refs[len(groups):]
    accs, (p_ref, ds_ref) = refs[:sides], refs[sides:]
    pays = [(ref, i) for ref, n in zip(pay_refs, sizes) for i in range(n)]
    dq_ins = [(ref, i) for ref, n in zip(dq_in_refs, dq_sizes) for i in range(n)]
    rows = kvs[0].shape[1]
    blocks = rows // LANES

    def row_of(aux, kind):
        return jnp.concatenate([aux[kind * blocks + j:kind * blocks + j + 1] for j in range(blocks)], axis=1)

    at = 2 * heads * rows
    auxes = []
    for ref, i in pays:
        aux = ref[i, at:, :].astype(F32)
        auxes.append(aux[0:16] + aux[16:32] + aux[32:48])
    for h in range(heads):
        cols = slice(h * LANES, (h + 1) * LANES)
        q = jnp.concatenate([ref[i, h * rows:(h + 1) * rows, :] for ref, i in pays], axis=0)
        do = jnp.concatenate([ref[i, (heads + h) * rows:(heads + h + 1) * rows, :] for ref, i in pays], axis=0)
        log = jnp.concatenate([row_of(aux, h) for aux in auxes], axis=1)
        delta = jnp.concatenate([row_of(aux, heads + h) for aux in auxes], axis=1)
        log = log * LOG2_E
        turned = []
        for s in range(sides):
            k = kvs[s][0, :, cols]
            v = kvs[s][1, :, cols]
            for start in range(0, q.shape[0], CHUNK):
                part = slice(start, min(start + CHUNK, q.shape[0]))
                p = jnp.exp2(dot(k, q[part], NT) * (scale * LOG2_E) - log[:, part])
                ds = p * (dot(v, do[part], NT) - delta[:, part])
                p_ref[h * sides + s, :, part] = p.astype(BF16)
                ds_ref[h * sides + s, :, part] = ds.astype(BF16)
            p = p_ref[h * sides + s]
            ds = ds_ref[h * sides + s]
            dv = dot(p, do)
            dk = dot(ds, q)
            if more_acc:
                dv = dv + acc_ins[s][1, :, cols]
                dk = dk + acc_ins[s][0, :, cols]
            accs[s][1, :, cols] = dv.astype(accs[s].dtype)
            accs[s][0, :, cols] = dk.astype(accs[s].dtype)
            turned.append(k.astype(F32).T.astype(BF16))
        all_ds = ds_ref[h * sides:(h + 1) * sides].reshape(sides * rows, q.shape[0])
        dq = dot(jnp.concatenate(turned, axis=1), all_ds)
        for out, group in zip(dqs, groups):
            for at_out, tile in enumerate(group):
                mine = dq[:, tile * rows:(tile + 1) * rows]
                if dq_ins:
                    ref, i = dq_ins[tile]
                    mine = mine + ref[i, cols, :]
                out[at_out, cols, :] = mine.astype(out.dtype)


def run_tiles(pays, kvs, heads, scale, groups, kinds, acc_kinds, dq_in=(), acc_in=(), weight=1):
    sizes = [pay.shape[0] for pay in pays]
    _, rows, width = kvs[0].shape
    here = pl.BlockSpec(memory_space=pltpu.VMEM)
    done = pl.pallas_call(
        functools.partial(
            tiles_kernel, sizes, len(kvs), heads, scale, [x.shape[0] for x in dq_in], bool(acc_in), groups
        ),
        in_specs=[here] * (len(pays) + len(kvs) + len(dq_in) + len(acc_in)),
        out_specs=[here] * (len(groups) + len(kvs)),
        out_shape=[jax.ShapeDtypeStruct((len(group), width, rows), kind) for group, kind in zip(groups, kinds)]
        + [jax.ShapeDtypeStruct((2, rows, width), kind) for kind in acc_kinds],
        scratch_shapes=[pltpu.VMEM((heads * len(kvs), rows, sum(sizes) * rows), BF16)] * 2,
        compiler_params=pltpu.CompilerParams(vmem_limit_bytes=VMEM_BYTES),
        cost_estimate=pl.CostEstimate(
            flops=weight * 10 * sum(sizes) * len(kvs) * rows * rows * width, bytes_accessed=0, transcendentals=0
        ),
        name="tiles",
    )(*pays, *kvs, *dq_in, *acc_in)
    return done[:len(groups)], done[len(groups):]


def finish_kernel(scale, dq_ref, a_ref, b_ref, row_a_ref, row_b_ref, dkv_ref, dkv_a_ref, dkv_b_ref, q_out, k_out, v_out):
    dkv = [dkv_ref[i] + dkv_a_ref[i].astype(F32) + dkv_b_ref[i].astype(F32) for i in range(2)]
    k_out[...] = (dkv[0] * scale).astype(BF16)
    v_out[...] = dkv[1].astype(BF16)
    dq = dq_ref[0]
    for ref in (a_ref, b_ref, row_a_ref, row_b_ref):
        dq = dq + ref[0].astype(F32)
    q_out[...] = (dq * scale).T.astype(BF16)


def finish(dq, a, b, row_a, row_b, dkv, dkv_a, dkv_b, scale):
    _, rows, width = dkv.shape
    return pl.pallas_call(
        functools.partial(finish_kernel, scale),
        out_shape=[jax.ShapeDtypeStruct((rows, width), BF16)] * 3,
        compiler_params=pltpu.CompilerParams(vmem_limit_bytes=VMEM_BYTES),
        name="finish",
    )(dq, a, b, row_a, row_b, dkv, dkv_a, dkv_b)


def local(queries, key_vectors, value_vectors, forward_out, cotangent, log_norm):
    rows, width = queries.shape[3:]
    heads = log_norm.shape[3]
    scale = (width // heads) ** (-0.5)
    flat = (rows, width)
    own, own_kv = make_payloads(
        queries.reshape(flat),
        cotangent.reshape(flat),
        forward_out.reshape(flat),
        log_norm.reshape(heads, rows),
        key_vectors.reshape(flat),
        value_vectors.reshape(flat),
    )

    kv_b = meet(own_kv, "col", 1)
    kv_a = meet(own_kv, "col", 0)
    row_b = meet(own, "row", 1)
    row_a = meet(own, "row", 0)
    frame_b = meet(own, "frame", 1)
    frame_a = meet(own, "frame", 0)
    pair = jnp.concatenate([row_a, row_b], axis=0)
    pair_b = meet(pair, "frame", 1)
    pair_a = meet(pair, "frame", 0)

    work = functools.partial(run_tiles, heads=heads, scale=scale)
    near = [own, row_a, row_b, frame_a, frame_b]
    far = [pair_a, pair_b]
    near_dqs, accs = work(
        near, [own_kv, kv_a], groups=[[0], [1], [2], [3], [4]], kinds=[F32] * 5, acc_kinds=[F32] * 2, weight=3
    )
    far_dqs, (dkv, to_a) = work(
        far, [own_kv, kv_a], acc_in=accs, groups=[[0, 1], [2, 3]], kinds=[F32] * 2, acc_kinds=[F32, BF16], weight=0
    )
    (dq_own, dq_row_a, dq_row_b, dq_frame_b, dq_frame_a), (to_b,) = work(
        near + far,
        [kv_b],
        dq_in=[*near_dqs, *far_dqs],
        groups=[[0], [1], [2], [4, 7, 8], [3, 5, 6]],
        kinds=[F32] * 3 + [BF16] * 2,
        acc_kinds=[BF16],
        weight=0,
    )

    dkv_b = meet(to_b, "col", 1)
    dkv_a = meet(to_a, "col", 0)
    back_b = meet(dq_frame_b, "frame", 1)
    back_a = meet(dq_frame_a, "frame", 0)
    back = back_a.astype(F32) + back_b.astype(F32)
    row_back_b = meet((dq_row_b + back[2:3]).astype(BF16), "row", 1)
    row_back_a = meet((dq_row_a + back[1:2]).astype(BF16), "row", 0)
    grads = finish(dq_own, back_b, back_a, row_back_a, row_back_b, dkv, dkv_a, dkv_b, scale)
    return tuple(grad.reshape(queries.shape) for grad in grads)


def solution(mesh):
    placed = P("frame", "row", "col", None, None)
    return jax.shard_map(
        local,
        mesh=mesh,
        in_specs=(placed,) * 6,
        out_specs=(placed,) * 3,
        check_vma=False,
    )
```
